32 devices in a mesh: rec: 8 (over y, x, core), chan: 4 (over z).
Axes of the slice: x: 2, y: 2, z: 4, core: 2. Of those that a mesh axis runs over, the one named last changes fastest.
Arguments:
- signal: bfloat16 [4, 32, 307200], P(None, 'chan', 'rec'), may hold values from -6 to 6
- montage: int32 [4, 4, 8], P(None, 'chan'), may hold values from 0 to 7, each once within a row
- channels: int32 [4], replicated, may hold values from 19 to 32
- lengths: int32 [4], replicated, may hold values from 769 to 1536
- boundary: int32 [4, 1536], P(None, 'rec'), may hold values 0 or 1
- conv_in: bfloat16 [8, 4, 5, 200, 128], P('rec', 'chan'), may hold values from -0.1875 to 0.1875
- conv_hid: bfloat16 [8, 4, 2, 5, 128, 128], P('rec', 'chan'), may hold values from -0.25 to 0.25
- mix_weight: bfloat16 [8, 4, 128, 512], P(None, 'chan'), may hold values from -0.09375 to 0.09375
- norm_gain: float32 [512], replicated, may hold values from 0.1 to 1.9
- emit_weight: float32 [512, 5], replicated, may hold values from -1 to 1
- trans_within: float32 [5, 5], replicated, may hold values from -3 to 3
- trans_between: float32 [5, 5], replicated, may hold values from -2 to 102
- initial: float32 [5], replicated, may hold values from -6 to 6
Outputs:
- filtered: float32 [4, 5, 1536], P(None, None, 'rec')
- log_rate: float32 [4], replicated
The draws below stay inside these ranges and needn't reach their ends.
All inputs are finite; a program needn't handle non-finite values. No bound on the sum of `boundary` on one device may be relied on, other than what follows from the above.
Results may differ from the reference program's by a relative error of at most 0.011.
Values may be sent and summed in bfloat16 or wider, within the bound.
A program may use at most 128 MiB of HBM per device.

```python
import jax
import jax.numpy as jnp
from jax import lax

SAMP = 200
EMB = 128
MIX = 512
TAPS = 5
LAYERS = 2
STATES = 5
RECS = 4
GROUP = 8
TYPES = 32
NPATCH = 1536
NSAMP = 307200
N_CHAN = 4


def draw_trans_within(key, part):
    keys = jax.random.split(key, 2)
    diagonal_part = jax.random.uniform(keys[0], (STATES, STATES), jnp.float32, 1.0, 3.0)
    off_part = jax.random.uniform(keys[1], (STATES, STATES), jnp.float32, -3.0, -0.5)
    identity = jnp.eye(STATES, dtype=jnp.float32)
    return identity * diagonal_part + (1.0 - identity) * off_part


def draw_trans_between(key, part):
    base_values = jax.random.uniform(key, (STATES, STATES), jnp.float32, -2.0, 2.0)
    return base_values


def plant(values, key, low, largest):
    spot = [jax.random.randint(jax.random.fold_in(key, axis), (), 0, length) for axis, length in enumerate(values.shape)]
    longest = values.shape.index(max(values.shape))
    neighbour = spot[:longest] + [(spot[longest] + 1) % values.shape[longest]] + spot[longest + 1:]
    return values.at[tuple(spot)].set(low).at[tuple(neighbour)].set(largest)


def block_scale(key, extent, shards, smallest, largest):
    factor_of = 1.0
    for dim, blocks in shards:
        steps = jax.random.uniform(jax.random.fold_in(jax.random.fold_in(key, 6), dim), (blocks,), jnp.float32, smallest / len(shards), largest / len(shards))
        factor_of = factor_of * jnp.repeat(jnp.exp(steps), extent[dim] // blocks).reshape((-1,) + (1,) * (len(extent) - 1 - dim))
    return factor_of


def noise(rng, dims, spread, bound, cuts=(), kind=jnp.bfloat16):
    factor_of = block_scale(rng, dims, cuts, -0.22, 0.18) if cuts else 1.0
    values = jax.random.normal(rng, dims, jnp.float32) * spread * factor_of
    return jnp.minimum(jnp.maximum(values, -bound), bound).astype(kind)


def setup_inputs(seed: int = 0) -> dict:
    arg_keys = jax.random.split(jax.random.key(seed), 14)
    signal = noise(arg_keys[0], (RECS, TYPES, NSAMP), 1.0, 6.0, ((1, 4), (2, 8)))
    montage = jax.vmap(lambda own: jax.random.permutation(own, GROUP))(jax.random.split(arg_keys[1], RECS * N_CHAN)).reshape((RECS, N_CHAN, GROUP)).astype(jnp.int32)
    channels = plant(jax.random.randint(arg_keys[2], (RECS,), 19, TYPES + 1), jax.random.fold_in(arg_keys[2], 1), 19, TYPES).astype(jnp.int32)
    lengths = plant(jax.random.randint(arg_keys[3], (RECS,), NPATCH // 2 + 1, NPATCH + 1), jax.random.fold_in(arg_keys[3], 1), NPATCH // 2 + 1, NPATCH).astype(jnp.int32)
    boundary = plant((jax.random.randint(arg_keys[4], (RECS, NPATCH), 0, 8) < 1).astype(jnp.int32), jax.random.fold_in(arg_keys[4], 1), 0, 1)
    conv_in = noise(arg_keys[5], (GROUP, N_CHAN, TAPS, SAMP, EMB), (TAPS * SAMP) ** -0.5, 0.1875, ((0, 8), (1, 4)))
    conv_hid = noise(arg_keys[6], (GROUP, N_CHAN, LAYERS, TAPS, EMB, EMB), (TAPS * EMB) ** -0.5, 0.25, ((0, 8), (1, 4)))
    mix_weight = noise(arg_keys[7], (GROUP, N_CHAN, EMB, MIX), (TYPES * EMB) ** -0.5, 0.09375, ((1, 4),))
    norm_gain = jnp.clip(1.0 + 0.18 * jax.random.normal(arg_keys[8], (MIX,), jnp.float32), 0.1, 1.9)
    emit_weight = noise(arg_keys[9], (MIX, STATES), (MIX // 16) ** -0.5, 1.0, (), jnp.float32)
    trans_within = draw_trans_within(jax.random.fold_in(arg_keys[13], 71), 0)
    trans_between = draw_trans_between(jax.random.fold_in(arg_keys[13], 71), 0)
    initial = noise(arg_keys[12], (STATES,), 1.5, 6.0, (), jnp.float32)
    return {"signal": signal, "montage": montage, "channels": channels, "lengths": lengths, "boundary": boundary, "conv_in": conv_in, "conv_hid": conv_hid, "mix_weight": mix_weight, "norm_gain": norm_gain, "emit_weight": emit_weight, "trans_within": trans_within, "trans_between": trans_between, "initial": initial}


EPSILON = 1e-05

def log_sum_exp(values, along):
    peak_value = lax.optimization_barrier(jnp.max(values, axis=along, keepdims=True))
    return jnp.squeeze(peak_value, along) + jnp.log(lax.optimization_barrier(jnp.sum(jnp.exp(values - peak_value), axis=along)))

def temporal(patch_rows, taps):
    row_count, length, in_width = patch_rows.shape
    half_taps = taps.shape[0] // 2
    padded = jnp.pad(patch_rows, ((0, 0), (half_taps, half_taps), (0, 0)))
    accumulated = jnp.zeros((row_count * length, taps.shape[2]), jnp.float32)
    for offset in range(taps.shape[0]):
        window = padded[:, offset:offset + length].reshape(row_count * length, in_width)
        accumulated = accumulated + jnp.dot(window, taps[offset], preferred_element_type=jnp.float32)
    return accumulated.reshape(row_count, length, taps.shape[2])

def conv_stack(patch_rows, first_taps, hidden_taps):
    current = jax.nn.gelu(temporal(patch_rows, first_taps)).astype(jnp.bfloat16)
    for depth_index in range(hidden_taps.shape[0]):
        update = jax.nn.gelu(temporal(current, hidden_taps[depth_index]))
        current = (current.astype(jnp.float32) + update).astype(jnp.bfloat16)
    return current

def reference(signal, montage, channels, lengths, boundary, conv_in, conv_hid, mix_weight, norm_gain, emit_weight, trans_within, trans_between, initial):
    slot_ids = jnp.arange(TYPES, dtype=jnp.int32)
    live_slots = slot_ids[None, :] < channels[:, None]
    cleaned = jnp.where(live_slots[:, :, None], signal, jnp.zeros((), jnp.bfloat16))
    cleaned = cleaned.reshape(RECS, N_CHAN, GROUP, NPATCH, SAMP)
    places = jnp.arange(GROUP, dtype=jnp.int32)
    matches = montage[:, :, :, None] == places[None, None, None, :]
    inverse = lax.optimization_barrier(jnp.sum(jnp.where(matches, places[None, None, :, None], 0), axis=2)).astype(jnp.int32)

    def one_type(mixed_sum, type_index):
        owner = type_index // N_CHAN
        column = type_index % N_CHAN
        group_rows = lax.dynamic_index_in_dim(cleaned, column, 1, keepdims=False)
        picked = lax.dynamic_index_in_dim(inverse, column, 1, keepdims=False)
        slot_pick = lax.dynamic_index_in_dim(picked, owner, 1, keepdims=False).astype(jnp.int32)
        patch_rows = jnp.take_along_axis(group_rows, slot_pick[:, None, None, None], axis=1)[:, 0]
        encoded = conv_stack(patch_rows, conv_in[owner, column], conv_hid[owner, column])
        mixed_sum = mixed_sum + jnp.dot(encoded.reshape(RECS * NPATCH, EMB), mix_weight[owner, column], preferred_element_type=jnp.float32)
        return (mixed_sum, None)
    mixed, _ = lax.scan(one_type, jnp.zeros((RECS * NPATCH, MIX), jnp.float32), jnp.arange(TYPES, dtype=jnp.int32))
    average = lax.optimization_barrier(jnp.mean(mixed, axis=-1, keepdims=True))
    centred = mixed - average
    variance = lax.optimization_barrier(jnp.mean(centred * centred, axis=-1, keepdims=True))
    activated = jax.nn.gelu(centred * lax.rsqrt(variance + EPSILON) * norm_gain)
    emission = jnp.dot(activated, emit_weight, precision=lax.Precision.HIGHEST).reshape(RECS, NPATCH, STATES)
    prior = initial - log_sum_exp(initial, 0)
    start_state = jnp.broadcast_to(prior, (RECS, STATES))
    positions = jnp.arange(NPATCH, dtype=jnp.int32)
    valid = positions[None, :] < lengths[:, None]
    cross = boundary == 1

    def advance(carried, inputs):
        current, running = carried
        emit_now, cross_now, valid_now = inputs
        transition = jnp.where(cross_now[:, None, None], trans_between[None], trans_within[None])
        moved = log_sum_exp(current[:, :, None] + transition, 1) + emit_now
        log_level = log_sum_exp(moved, 1)
        current = jnp.where(valid_now[:, None], moved - log_level[:, None], current)
        running = running + jnp.where(valid_now, log_level, jnp.zeros_like(log_level))
        return ((current, running), current)
    (last_state, running), history = lax.scan(advance, (start_state, jnp.zeros((RECS,), jnp.float32)), (jnp.transpose(emission, (1, 0, 2)), cross.T, valid.T))
    filtered = jnp.transpose(history, (1, 2, 0))
    log_rate = running / lengths.astype(jnp.float32)
    return (filtered, log_rate)
```

```python
import jax
import jax.numpy as jnp
from jax import lax
from jax.experimental import pallas as pl
from jax.experimental.pallas import tpu as pltpu
from jax.sharding import PartitionSpec as P

SAMP = 200
EMB = 128
STATES = 5


EPSILON = 1e-05
NEGATIVE = -1e30


def temporal(patch_rows, taps):
    row_count, length, in_width = patch_rows.shape
    half_taps = taps.shape[0] // 2
    padded = jnp.pad(patch_rows, ((0, 0), (half_taps, half_taps), (0, 0)))
    accumulated = jnp.zeros((row_count * length, taps.shape[2]), jnp.float32)
    for offset in range(taps.shape[0]):
        window = padded[:, offset : offset + length].reshape(row_count * length, in_width)
        accumulated = accumulated + jnp.dot(
            window, taps[offset], preferred_element_type=jnp.float32
        )
    return accumulated.reshape(row_count, length, taps.shape[2])


def conv_stack(patch_rows, first_taps, hidden_taps):
    current = jax.nn.gelu(temporal(patch_rows, first_taps)).astype(jnp.bfloat16)
    for depth_index in range(hidden_taps.shape[0]):
        update = jax.nn.gelu(temporal(current, hidden_taps[depth_index]))
        current = (current.astype(jnp.float32) + update).astype(jnp.bfloat16)
    return current


LANES = 128


def lse_list(terms):
    peak = terms[0]
    for term in terms[1:]:
        peak = jnp.maximum(peak, term)
    total = jnp.exp(terms[0] - peak)
    for term in terms[1:]:
        total = total + jnp.exp(term - peak)
    return peak + jnp.log(total)


def peak_of(matrix):
    peak = matrix[0]
    for entry in matrix[1:]:
        peak = jnp.maximum(peak, entry)
    return peak


def crf_kernel(
    field_ref, length_ref, within_ref, between_ref, initial_ref, filtered_ref, total_ref
):
    steps, recordings = field_ref.shape[1], field_ref.shape[2]
    shape = (recordings, LANES)
    lane = lax.broadcasted_iota(jnp.int32, shape, 1)
    length = length_ref[...]
    states = range(STATES)
    identity = [jnp.full(shape, 0.0 if i == s else NEGATIVE) for i in states for s in states]

    def transition(step):
        cross = field_ref[STATES, step] > 0.5
        return [
            jnp.where(cross, between_ref[i, s], within_ref[i, s]) for i in states for s in states
        ]

    def grow(step, matrix):
        moves = transition(step)
        valid = lane * steps + step < length
        grown = []
        for i in states:
            for s in states:
                moved = lse_list([matrix[i * STATES + k] + moves[k * STATES + s] for k in states])
                grown.append(
                    jnp.where(valid, moved + field_ref[s, step], matrix[i * STATES + s])
                )
        return tuple(grown)

    moves = transition(0)
    valid = lane * steps < length
    matrix = tuple(
        jnp.where(valid, moves[i * STATES + s] + field_ref[s, 0], identity[i * STATES + s])
        for i in states
        for s in states
    )
    matrix = lax.fori_loop(1, steps, grow, matrix)
    offset = peak_of(matrix)
    matrix = [entry - offset for entry in matrix]
    distance = 1
    while distance < LANES:
        inside = lane >= distance
        before = [
            jnp.where(inside, pltpu.roll(entry, distance, 1), unit)
            for entry, unit in zip(matrix, identity)
        ]
        offset = offset + jnp.where(inside, pltpu.roll(offset, distance, 1), 0.0)
        product = [
            lse_list([before[i * STATES + k] + matrix[k * STATES + s] for k in states])
            for i in states
            for s in states
        ]
        peak = peak_of(product)
        matrix = [entry - peak for entry in product]
        offset = offset + peak
        distance *= 2
    prior = [jnp.full(shape, initial_ref[s]) for s in states]
    level = lse_list(prior)
    prior = [entry - level for entry in prior]
    reached = [lse_list([prior[i] + matrix[i * STATES + s] for i in states]) for s in states]
    level = lse_list(reached)
    total_ref[...] = level + offset
    start = tuple(
        jnp.where(lane >= 1, pltpu.roll(entry - level, 1, 1), unit)
        for entry, unit in zip(reached, prior)
    )

    def advance(step, vector):
        moves = transition(step)
        valid = lane * steps + step < length
        moved = [
            lse_list([vector[i] + moves[i * STATES + s] for i in states]) + field_ref[s, step]
            for s in states
        ]
        height = lse_list(moved)
        vector = tuple(
            jnp.where(valid, entry - height, old) for entry, old in zip(moved, vector)
        )
        for s in states:
            filtered_ref[step, s] = vector[s]
        return vector

    lax.fori_loop(0, steps, advance, start)


def crf(field, lengths, within, between, initial):
    steps, recordings = field.shape[1], field.shape[2]
    vmem = pl.BlockSpec(memory_space=pltpu.VMEM)
    smem = pl.BlockSpec(memory_space=pltpu.SMEM)
    return pl.pallas_call(
        crf_kernel,
        out_shape=(
            jax.ShapeDtypeStruct((steps, STATES, recordings, LANES), jnp.float32),
            jax.ShapeDtypeStruct((recordings, LANES), jnp.float32),
        ),
        in_specs=[vmem, vmem, smem, smem, smem],
        out_specs=(vmem, vmem),
    )(
        field,
        jnp.broadcast_to(lengths[:, None], (recordings, LANES)),
        within,
        between,
        initial,
    )


def finish(
    partial, boundary, lengths, norm_gain, emit_weight, trans_within, trans_between, initial
):
    groups = lax.axis_size("rec")
    columns = lax.axis_size("chan")
    rec_index = lax.axis_index("rec")
    chan_index = lax.axis_index("chan")
    recordings, patches = boundary.shape
    rows = recordings * patches // columns
    pieces = partial.reshape(columns, rows, partial.shape[-1])
    pieces = lax.all_to_all(pieces.astype(jnp.bfloat16), "chan", 0, 0, tiled=True)
    summed = jnp.sum(pieces.astype(jnp.float32), axis=0)
    average = jnp.mean(summed, axis=-1, keepdims=True)
    centred = summed - average
    variance = jnp.mean(centred * centred, axis=-1, keepdims=True)
    activated = jax.nn.gelu(centred * lax.rsqrt(variance + EPSILON) * norm_gain)
    emission = jnp.einsum("ro,os->sr", activated, emit_weight, precision=lax.Precision.HIGHEST)
    cross = lax.dynamic_slice_in_dim(boundary.reshape(-1), chan_index * rows, rows)
    field = jnp.concatenate([emission, (cross == 1).astype(jnp.float32)[None]], axis=0)
    field = lax.all_gather(field, ("rec", "chan"))
    wide = LANES // groups
    steps = patches // wide
    field = field.reshape(groups, columns, STATES + 1, rows)
    field = jnp.transpose(field, (0, 2, 1, 3)).reshape(
        groups, STATES + 1, recordings, wide, steps
    )
    field = jnp.transpose(field, (1, 4, 2, 0, 3)).reshape(STATES + 1, steps, recordings, LANES)
    history, total = crf(field, lengths, trans_within, trans_between, initial)
    own = lax.dynamic_slice_in_dim(history, rec_index * wide, wide, axis=3)
    filtered = jnp.transpose(own, (2, 1, 3, 0)).reshape(recordings, STATES, patches)
    return filtered, total[:, LANES - 1] / lengths.astype(jnp.float32)


def local(
    signal,
    montage,
    channels,
    lengths,
    boundary,
    conv_in,
    conv_hid,
    mix_weight,
    norm_gain,
    emit_weight,
    trans_within,
    trans_between,
    initial,
):
    groups = lax.axis_size("rec")
    chan_index = lax.axis_index("chan")
    recordings = signal.shape[0]
    patches = signal.shape[2] // SAMP
    slot_ids = chan_index * groups + jnp.arange(groups, dtype=jnp.int32)
    live_slots = slot_ids[None, :] < channels[:, None]
    cleaned = jnp.where(live_slots[:, :, None], signal, jnp.zeros((), jnp.bfloat16))
    places = jnp.arange(groups, dtype=jnp.int32)
    matches = montage[:, 0, :, None] == places[None, None, :]
    inverse = jnp.sum(jnp.where(matches, places[None, :, None], 0), axis=1)
    outgoing = jnp.take_along_axis(cleaned, inverse[:, :, None], axis=1)
    received = lax.all_to_all(outgoing, "rec", split_axis=1, concat_axis=1, tiled=True)
    item_count = received.shape[0]
    patch_rows = received.reshape(item_count, groups * patches, SAMP)
    encoded = conv_stack(patch_rows, conv_in[0, 0], conv_hid[0, 0])
    shards = encoded.reshape(item_count, groups, patches, EMB)
    arrived = shards
    arrived = lax.all_to_all(arrived, "rec", split_axis=1, concat_axis=1, tiled=True)
    partial_value = jnp.einsum(
        "bkpe,keo->bpo", arrived, mix_weight[:, 0], preferred_element_type=jnp.float32
    )
    return finish(
        partial_value,
        boundary,
        lengths,
        norm_gain,
        emit_weight,
        trans_within,
        trans_between,
        initial,
    )


def solution(mesh):
    placed = (
        P(None, "chan", "rec"),
        P(None, "chan", None),
        P(),
        P(),
        P(None, "rec"),
        P("rec", "chan", None, None, None),
        P("rec", "chan", None, None, None, None),
        P(None, "chan", None, None),
        P(),
        P(),
        P(),
        P(),
        P(),
    )
    return jax.shard_map(
        local, mesh=mesh, in_specs=placed, out_specs=(P(None, None, "rec"), P()), check_vma=False
    )
```

```python
import functools

import jax
import jax.numpy as jnp
from jax import lax
from jax.experimental import pallas as pl
from jax.experimental.pallas import tpu as pltpu
from jax.sharding import PartitionSpec as P

SAMP = 200
EMB = 128
STATES = 5


EPSILON = 1e-05
NEGATIVE = -1e30


LANES = 128


def lse_list(terms):
    peak = terms[0]
    for term in terms[1:]:
        peak = jnp.maximum(peak, term)
    total = jnp.exp(terms[0] - peak)
    for term in terms[1:]:
        total = total + jnp.exp(term - peak)
    return peak + jnp.log(total)


def peak_of(matrix):
    peak = matrix[0]
    for entry in matrix[1:]:
        peak = jnp.maximum(peak, entry)
    return peak


def crf_kernel(
    field_ref, length_ref, within_ref, between_ref, initial_ref, filtered_ref, total_ref
):
    steps, recordings = field_ref.shape[1], field_ref.shape[2]
    shape = (recordings, LANES)
    lane = lax.broadcasted_iota(jnp.int32, shape, 1)
    length = length_ref[...]
    states = range(STATES)
    identity = [jnp.full(shape, 0.0 if i == s else NEGATIVE) for i in states for s in states]

    def transition(step):
        cross = field_ref[STATES, step] > 0.5
        return [
            jnp.where(cross, between_ref[i, s], within_ref[i, s]) for i in states for s in states
        ]

    def grow(step, matrix):
        moves = transition(step)
        valid = lane * steps + step < length
        grown = []
        for i in states:
            for s in states:
                moved = lse_list([matrix[i * STATES + k] + moves[k * STATES + s] for k in states])
                grown.append(
                    jnp.where(valid, moved + field_ref[s, step], matrix[i * STATES + s])
                )
        return tuple(grown)

    moves = transition(0)
    valid = lane * steps < length
    matrix = tuple(
        jnp.where(valid, moves[i * STATES + s] + field_ref[s, 0], identity[i * STATES + s])
        for i in states
        for s in states
    )
    matrix = lax.fori_loop(1, steps, grow, matrix)
    offset = peak_of(matrix)
    matrix = [entry - offset for entry in matrix]
    distance = 1
    while distance < LANES:
        inside = lane >= distance
        before = [
            jnp.where(inside, pltpu.roll(entry, distance, 1), unit)
            for entry, unit in zip(matrix, identity)
        ]
        offset = offset + jnp.where(inside, pltpu.roll(offset, distance, 1), 0.0)
        product = [
            lse_list([before[i * STATES + k] + matrix[k * STATES + s] for k in states])
            for i in states
            for s in states
        ]
        peak = peak_of(product)
        matrix = [entry - peak for entry in product]
        offset = offset + peak
        distance *= 2
    prior = [jnp.full(shape, initial_ref[s]) for s in states]
    level = lse_list(prior)
    prior = [entry - level for entry in prior]
    reached = [lse_list([prior[i] + matrix[i * STATES + s] for i in states]) for s in states]
    level = lse_list(reached)
    total_ref[...] = level + offset
    start = tuple(
        jnp.where(lane >= 1, pltpu.roll(entry - level, 1, 1), unit)
        for entry, unit in zip(reached, prior)
    )

    def advance(step, vector):
        moves = transition(step)
        valid = lane * steps + step < length
        moved = [
            lse_list([vector[i] + moves[i * STATES + s] for i in states]) + field_ref[s, step]
            for s in states
        ]
        height = lse_list(moved)
        vector = tuple(
            jnp.where(valid, entry - height, old) for entry, old in zip(moved, vector)
        )
        for s in states:
            filtered_ref[step, s] = vector[s]
        return vector

    lax.fori_loop(0, steps, advance, start)


def crf(field, lengths, within, between, initial):
    steps, recordings = field.shape[1], field.shape[2]
    vmem = pl.BlockSpec(memory_space=pltpu.VMEM)
    smem = pl.BlockSpec(memory_space=pltpu.SMEM)
    return pl.pallas_call(
        crf_kernel,
        out_shape=(
            jax.ShapeDtypeStruct((steps, STATES, recordings, LANES), jnp.float32),
            jax.ShapeDtypeStruct((recordings, LANES), jnp.float32),
        ),
        in_specs=[vmem, vmem, smem, smem, smem],
        out_specs=(vmem, vmem),
    )(
        field,
        jnp.broadcast_to(lengths[:, None], (recordings, LANES)),
        within,
        between,
        initial,
    )


MESH = pl.DeviceIdType.MESH
VMEM_LIMIT = 52 * 1024 * 1024
HALO = 8
DEPTH = 208


def vmem_spec():
    return pl.BlockSpec(memory_space=pltpu.VMEM)


def cut_kernel(pick_ref, live_ref, signal_ref, left_ref, right_ref, rows_ref, low_ref, high_ref):
    lines = signal_ref.shape[0]
    types, total = rows_ref.shape[0], rows_ref.shape[1]
    recordings = pick_ref.shape[0]
    length = total // recordings
    patches = length - 2 * HALO
    reach = left_ref.shape[1]
    live = live_ref[...] > 0

    def put(chunk, offset, row):
        piece = chunk[:, offset : offset + SAMP]
        low_ref[pl.ds(row * lines, lines), :] = piece[:, :128]
        high_ref[pl.ds(row * lines, lines), :] = jnp.concatenate(
            [piece[:, 128:], jnp.zeros((lines, 256 - SAMP), jnp.float32)], axis=1
        )

    def kept(block):
        return jnp.where(live, block.astype(jnp.float32), 0.0)

    blank = jnp.zeros((2 * lines, 128), jnp.float32)
    for part in (low_ref, high_ref):
        part[pl.ds(0, 2 * lines), :] = blank
        part[pl.ds((length - 2) * lines, 2 * lines), :] = blank
    left = kept(left_ref[...])
    right = kept(right_ref[...])
    for q in range(6):
        put(left, reach - (6 - q) * SAMP, 2 + q)
        put(right, q * SAMP, HALO + patches + q)
    period = 16

    def cut(step, carry):
        start = pl.multiple_of(step * (period * SAMP), 128)
        block = kept(signal_ref[:, pl.ds(start, period * SAMP)])
        for q in range(period):
            put(block, q * SAMP, HALO + step * period + q)
        return carry

    lax.fori_loop(0, patches // period, cut, 0)

    def pick(item, carry):
        kind, recording = item // recordings, item % recordings
        line = recording * types + pick_ref[recording, kind]
        place = pl.ds(pl.multiple_of(recording * length, 16), length)
        low = low_ref[pl.ds(line, length, stride=lines), :]
        high = high_ref[pl.ds(line, length, stride=lines), :]
        rows_ref[kind, place, 0:128] = low.astype(jnp.bfloat16)
        rows_ref[kind, place, 128:DEPTH] = high[:, : DEPTH - 128].astype(jnp.bfloat16)
        return carry

    lax.fori_loop(0, types * recordings, pick, 0)


def encode_kernel(
    recordings, rows_ref, taps_ref, mix_ref, out_ref, held, wide, encoded, send, relay, recv, local
):
    types, total = rows_ref.shape[0], rows_ref.shape[1]
    length = total // recordings
    patches = length - 2 * HALO
    half = types // 2
    me = lax.axis_index("rec")
    pair, parity = me // 2, me % 2
    partner = 2 * pair + (1 - parity)

    barrier = pltpu.get_barrier_semaphore()
    for d in range(1, half):
        peer = 2 * ((pair + half - d) % half) + parity
        pl.semaphore_signal(barrier, inc=1, device_id={"rec": peer}, device_id_type=MESH)
    pl.semaphore_signal(barrier, inc=1, device_id={"rec": partner}, device_id_type=MESH)
    pl.semaphore_wait(barrier, half)

    sends = []
    own = pltpu.make_async_remote_copy(
        src_ref=taps_ref,
        dst_ref=held.at[me],
        send_sem=send.at[0],
        recv_sem=recv.at[me],
        device_id={"rec": partner},
        device_id_type=MESH,
    )
    own.start()
    sends.append(own)
    for d in range(1, half):
        peer = 2 * ((pair + half - d) % half) + parity
        copy = pltpu.make_async_remote_copy(
            src_ref=taps_ref,
            dst_ref=held.at[me],
            send_sem=send.at[d],
            recv_sem=recv.at[me],
            device_id={"rec": peer},
            device_id_type=MESH,
        )
        copy.start()
        sends.append(copy)
    keep = pltpu.make_async_copy(taps_ref, held.at[me], local)
    keep.start()
    edge = jnp.zeros((8, wide.shape[2]), jnp.float32)
    for slot in range(2):
        wide[slot, 0:8, :] = edge
        wide[slot, 8 + length : 16 + length, :] = edge
    position = lax.broadcasted_iota(jnp.int32, (length, EMB), 0) - HALO + me * patches
    inside = jnp.logical_and(position >= 0, position < types * patches)
    keep.wait()

    def conv(values, weights, slot):
        wide[slot, 8 : 8 + length, :] = jnp.dot(
            values, weights, preferred_element_type=jnp.float32
        )
        taps = weights.shape[1] // EMB
        first = 8 - taps // 2
        result = wide[slot, first : first + length, 0:EMB]
        for k in range(1, taps):
            result = result + wide[slot, first + k : first + k + length, k * EMB : (k + 1) * EMB]
        return jax.nn.gelu(result)

    depth_count = (taps_ref.shape[0] - DEPTH) // EMB

    def encode(source):
        def one(recording, slot):
            start = pl.multiple_of(recording * length, 16)
            patch_rows = rows_ref[source, pl.ds(start, length), :]
            current = conv(patch_rows, held[source, 0:DEPTH, :], slot)
            current = jnp.where(inside, current, 0.0).astype(jnp.bfloat16)
            for layer in range(depth_count):
                base = DEPTH + layer * EMB
                update = conv(current, held[source, base : base + EMB, :], slot)
                current = current.astype(jnp.float32) + update
                current = jnp.where(inside, current, 0.0).astype(jnp.bfloat16)
            encoded[
                pl.ds(pl.multiple_of(recording * patches, 16), patches),
                pl.ds(pl.multiple_of(source * EMB, EMB), EMB),
            ] = current[HALO : HALO + patches]

        def two(step, carry):
            one(2 * step, 0)
            one(2 * step + 1, 1)
            return carry

        lax.fori_loop(0, recordings // 2, two, 0)

    def arrival(slot):
        return pltpu.make_async_remote_copy(
            src_ref=taps_ref,
            dst_ref=held.at[slot],
            send_sem=send.at[0],
            recv_sem=recv.at[slot],
            device_id={"rec": partner},
            device_id_type=MESH,
        )

    for h in range(half):
        near = 2 * ((pair + h) % half) + parity
        far = 2 * ((pair + h) % half) + (1 - parity)
        if h > 0:
            arrival(near).wait_recv()
            forward = pltpu.make_async_remote_copy(
                src_ref=held.at[near],
                dst_ref=held.at[near],
                send_sem=relay.at[h],
                recv_sem=recv.at[near],
                device_id={"rec": partner},
                device_id_type=MESH,
            )
            forward.start()
            sends.append(forward)
        encode(near)
        arrival(far).wait_recv()
        encode(far)

    block = 2 * EMB

    def mix(step, carry):
        rows = pl.ds(pl.multiple_of(step * block, block), block)
        out_ref[rows, :] = jnp.dot(
            encoded[rows, :], mix_ref[...], preferred_element_type=jnp.float32
        ).astype(jnp.bfloat16)
        return carry

    lax.fori_loop(0, recordings * patches // block, mix, 0)
    for copy in sends:
        copy.wait_send()


def tail_kernel(
    part_ref, gain_ref, head_ref, extra_ref, out_ref,
    landed, column, spread, send1, recv1, send2, recv2, send3, recv3,
):
    columns, rows = part_ref.shape[0], part_ref.shape[1]
    groups = out_ref.shape[0]
    mine, me = lax.axis_index("chan"), lax.axis_index("rec")
    barrier = pltpu.get_barrier_semaphore()
    for d in range(1, columns):
        pl.semaphore_signal(
            barrier, inc=1, device_id={"chan": (mine + d) % columns}, device_id_type=MESH
        )
    for d in range(1, groups):
        pl.semaphore_signal(
            barrier, inc=1, device_id={"rec": (me + d) % groups}, device_id_type=MESH
        )
    pl.semaphore_wait(barrier, columns + groups - 2)

    def scatter(d):
        peer = (mine + d) % columns
        return pltpu.make_async_remote_copy(
            src_ref=part_ref.at[peer],
            dst_ref=landed.at[d],
            send_sem=send1.at[d],
            recv_sem=recv1.at[d],
            device_id={"chan": peer},
            device_id_type=MESH,
        )

    def along_chan(d):
        return pltpu.make_async_remote_copy(
            src_ref=column.at[mine],
            dst_ref=column.at[mine],
            send_sem=send2.at[d],
            recv_sem=recv2.at[d],
            device_id={"chan": (mine + d) % columns},
            device_id_type=MESH,
        )

    def along_rec(d):
        return pltpu.make_async_remote_copy(
            src_ref=column,
            dst_ref=spread.at[me],
            send_sem=send3.at[d],
            recv_sem=recv3.at[d],
            device_id={"rec": (me + d) % groups},
            device_id_type=MESH,
        )

    for d in range(1, columns):
        scatter(d).start()
    summed = part_ref[mine].astype(jnp.float32)
    for d in range(1, columns):
        scatter(d).wait()
        summed = summed + landed[d].astype(jnp.float32)
    average = jnp.mean(summed, axis=-1, keepdims=True)
    centred = summed - average
    variance = jnp.mean(centred * centred, axis=-1, keepdims=True)
    activated = jax.nn.gelu(centred * lax.rsqrt(variance + EPSILON) * gain_ref[...])
    emission = lax.dot_general(
        head_ref[...],
        activated,
        (((1,), (1,)), ((), ())),
        precision=lax.Precision.HIGHEST,
        preferred_element_type=jnp.float32,
    )
    column[mine] = jnp.zeros(column.shape[1:], jnp.float32)
    column[mine, :, 0:rows] = emission + extra_ref[...]
    for d in range(1, columns):
        along_chan(d).start()
    for d in range(1, columns):
        along_chan(d).wait()
    for d in range(1, groups):
        along_rec(d).start()
    out_ref[me] = column[...]
    for d in range(1, groups):
        along_rec(d).wait()
        source = (me + groups - d) % groups
        out_ref[source] = spread[source]


def local(
    signal,
    montage,
    channels,
    lengths,
    boundary,
    conv_in,
    conv_hid,
    mix_weight,
    norm_gain,
    emit_weight,
    trans_within,
    trans_between,
    initial,
):
    groups = lax.axis_size("rec")
    columns = lax.axis_size("chan")
    chan_index = lax.axis_index("chan")
    rec_index = lax.axis_index("rec")
    recordings, _, samples = signal.shape
    patches = samples // SAMP
    features = mix_weight.shape[-1]
    reach = -(-6 * SAMP // 128) * 128
    lines = recordings * groups
    flat = signal.reshape(lines, samples)
    ahead = [(i, i + 1) for i in range(groups - 1)]
    back = [(i + 1, i) for i in range(groups - 1)]
    left = lax.ppermute(flat[:, samples - reach :], "rec", ahead)
    right = lax.ppermute(flat[:, :reach], "rec", back)
    slot_ids = chan_index * groups + jnp.arange(groups, dtype=jnp.int32)
    live = (slot_ids[None, :] < channels[:, None]).astype(jnp.int32).reshape(lines, 1)
    places = jnp.arange(groups, dtype=jnp.int32)
    matches = montage[:, 0, :, None] == places[None, None, :]
    inverse = jnp.sum(jnp.where(matches, places[None, :, None], 0), axis=1)
    length = patches + 2 * HALO
    patch_rows = pl.pallas_call(
        cut_kernel,
        out_shape=jax.ShapeDtypeStruct((groups, recordings * length, DEPTH), jnp.bfloat16),
        in_specs=[pl.BlockSpec(memory_space=pltpu.SMEM)] + [vmem_spec()] * 4,
        out_specs=vmem_spec(),
        scratch_shapes=[pltpu.VMEM((length * lines, 128), jnp.float32)] * 2,
        compiler_params=pltpu.CompilerParams(vmem_limit_bytes=VMEM_LIMIT),
    )(inverse, live, flat, left, right)

    first = jnp.transpose(conv_in[0, 0], (1, 0, 2)).reshape(SAMP, -1)
    hidden = jnp.transpose(conv_hid[0, 0], (0, 2, 1, 3)).reshape(-1, first.shape[1])
    blank = jnp.zeros((DEPTH - SAMP, first.shape[1]), jnp.bfloat16)
    taps = jnp.concatenate([first, blank, hidden], axis=0)
    partial = pl.pallas_call(
        functools.partial(encode_kernel, recordings),
        out_shape=jax.ShapeDtypeStruct((recordings * patches, features), jnp.bfloat16),
        in_specs=[vmem_spec()] * 3,
        out_specs=vmem_spec(),
        scratch_shapes=[
            pltpu.VMEM((groups,) + taps.shape, jnp.bfloat16),
            pltpu.VMEM((2, length + 16, taps.shape[1]), jnp.float32),
            pltpu.VMEM((recordings * patches, groups * EMB), jnp.bfloat16),
            pltpu.SemaphoreType.DMA((groups // 2,)),
            pltpu.SemaphoreType.DMA((groups // 2,)),
            pltpu.SemaphoreType.DMA((groups,)),
            pltpu.SemaphoreType.DMA,
        ],
        compiler_params=pltpu.CompilerParams(
            collective_id=0, has_side_effects=True, vmem_limit_bytes=VMEM_LIMIT
        ),
    )(patch_rows, taps, mix_weight[:, 0].reshape(groups * EMB, features))

    rows = recordings * patches // columns
    padded = -(-rows // 128) * 128
    cross = lax.dynamic_slice_in_dim(boundary.reshape(-1), chan_index * rows, rows)
    cross = (cross == 1).astype(jnp.float32)
    extra = jnp.pad(cross[None], ((STATES, 2), (0, 0)))
    head = jnp.pad(emit_weight.T, ((0, 8 - STATES), (0, 0)))
    field = pl.pallas_call(
        tail_kernel,
        out_shape=jax.ShapeDtypeStruct((groups, columns, 8, padded), jnp.float32),
        in_specs=[vmem_spec()] * 4,
        out_specs=vmem_spec(),
        scratch_shapes=[
            pltpu.VMEM((columns, rows, features), jnp.bfloat16),
            pltpu.VMEM((columns, 8, padded), jnp.float32),
            pltpu.VMEM((groups, columns, 8, padded), jnp.float32),
        ]
        + [pltpu.SemaphoreType.DMA((count,)) for count in (columns, columns) * 2 + (groups, groups)],
        compiler_params=pltpu.CompilerParams(
            collective_id=1, has_side_effects=True, vmem_limit_bytes=VMEM_LIMIT
        ),
    )(partial.reshape(columns, rows, features), norm_gain[None], head, extra)

    wide = LANES // groups
    steps = patches // wide
    field = field[:, :, : STATES + 1, :rows]
    field = jnp.transpose(field, (0, 2, 1, 3)).reshape(
        groups, STATES + 1, recordings, wide, steps
    )
    field = jnp.transpose(field, (1, 4, 2, 0, 3)).reshape(STATES + 1, steps, recordings, LANES)
    history, total = crf(field, lengths, trans_within, trans_between, initial)
    own = lax.dynamic_slice_in_dim(history, rec_index * wide, wide, axis=3)
    filtered = jnp.transpose(own, (2, 1, 3, 0)).reshape(recordings, STATES, patches)
    return filtered, total[:, LANES - 1] / lengths.astype(jnp.float32)


def solution(mesh):
    placed = (
        P(None, "chan", "rec"),
        P(None, "chan", None),
        P(),
        P(),
        P(None, "rec"),
        P("rec", "chan", None, None, None),
        P("rec", "chan", None, None, None, None),
        P(None, "chan", None, None),
        P(),
        P(),
        P(),
        P(),
        P(),
    )
    return jax.shard_map(
        local, mesh=mesh, in_specs=placed, out_specs=(P(None, None, "rec"), P()), check_vma=False
    )
```

```python
import jax
import jax.numpy as jnp
from jax import lax
from jax.experimental import pallas as pl
from jax.experimental.pallas import tpu as pltpu
from jax.sharding import PartitionSpec as P

SAMP = 200
EMB = 128
STATES = 5


EPSILON = 1e-05
NEGATIVE = -1e30


LANES = 128


def lse_list(terms):
    peak = terms[0]
    for term in terms[1:]:
        peak = jnp.maximum(peak, term)
    total = jnp.exp(terms[0] - peak)
    for term in terms[1:]:
        total = total + jnp.exp(term - peak)
    return peak + jnp.log(total)


def peak_of(matrix):
    peak = matrix[0]
    for entry in matrix[1:]:
        peak = jnp.maximum(peak, entry)
    return peak


def crf_kernel(
    field_ref, length_ref, within_ref, between_ref, initial_ref, filtered_ref, total_ref
):
    steps, recordings = field_ref.shape[1], field_ref.shape[2]
    shape = (recordings, LANES)
    lane = lax.broadcasted_iota(jnp.int32, shape, 1)
    length = length_ref[...]
    states = range(STATES)
    identity = [jnp.full(shape, 0.0 if i == s else NEGATIVE) for i in states for s in states]

    def transition(step):
        cross = field_ref[STATES, step] > 0.5
        return [
            jnp.where(cross, between_ref[i, s], within_ref[i, s]) for i in states for s in states
        ]

    def grow(step, matrix):
        moves = transition(step)
        valid = lane * steps + step < length
        grown = []
        for i in states:
            for s in states:
                moved = lse_list([matrix[i * STATES + k] + moves[k * STATES + s] for k in states])
                grown.append(
                    jnp.where(valid, moved + field_ref[s, step], matrix[i * STATES + s])
                )
        return tuple(grown)

    moves = transition(0)
    valid = lane * steps < length
    matrix = tuple(
        jnp.where(valid, moves[i * STATES + s] + field_ref[s, 0], identity[i * STATES + s])
        for i in states
        for s in states
    )
    matrix = lax.fori_loop(1, steps, grow, matrix)
    offset = peak_of(matrix)
    matrix = [entry - offset for entry in matrix]
    distance = 1
    while distance < LANES:
        inside = lane >= distance
        before = [
            jnp.where(inside, pltpu.roll(entry, distance, 1), unit)
            for entry, unit in zip(matrix, identity)
        ]
        offset = offset + jnp.where(inside, pltpu.roll(offset, distance, 1), 0.0)
        product = [
            lse_list([before[i * STATES + k] + matrix[k * STATES + s] for k in states])
            for i in states
            for s in states
        ]
        peak = peak_of(product)
        matrix = [entry - peak for entry in product]
        offset = offset + peak
        distance *= 2
    prior = [jnp.full(shape, initial_ref[s]) for s in states]
    level = lse_list(prior)
    prior = [entry - level for entry in prior]
    reached = [lse_list([prior[i] + matrix[i * STATES + s] for i in states]) for s in states]
    level = lse_list(reached)
    total_ref[...] = level + offset
    start = tuple(
        jnp.where(lane >= 1, pltpu.roll(entry - level, 1, 1), unit)
        for entry, unit in zip(reached, prior)
    )

    def advance(step, vector):
        moves = transition(step)
        valid = lane * steps + step < length
        moved = [
            lse_list([vector[i] + moves[i * STATES + s] for i in states]) + field_ref[s, step]
            for s in states
        ]
        height = lse_list(moved)
        vector = tuple(
            jnp.where(valid, entry - height, old) for entry, old in zip(moved, vector)
        )
        for s in states:
            filtered_ref[step, s] = vector[s]
        return vector

    lax.fori_loop(0, steps, advance, start)


def crf(field, lengths, within, between, initial):
    steps, recordings = field.shape[1], field.shape[2]
    vmem = pl.BlockSpec(memory_space=pltpu.VMEM)
    smem = pl.BlockSpec(memory_space=pltpu.SMEM)
    return pl.pallas_call(
        crf_kernel,
        out_shape=(
            jax.ShapeDtypeStruct((steps, STATES, recordings, LANES), jnp.float32),
            jax.ShapeDtypeStruct((recordings, LANES), jnp.float32),
        ),
        in_specs=[vmem, vmem, smem, smem, smem],
        out_specs=(vmem, vmem),
    )(
        field,
        jnp.broadcast_to(lengths[:, None], (recordings, LANES)),
        within,
        between,
        initial,
    )


MESH = pl.DeviceIdType.MESH
VMEM_LIMIT = 52 * 1024 * 1024
HALO = 8
DEPTH = 208


def vmem_spec():
    return pl.BlockSpec(memory_space=pltpu.VMEM)


def cut_rows(pick_ref, live_ref, signal_ref, left_ref, right_ref, rows_ref, low_ref, high_ref):
    lines = signal_ref.shape[0]
    types, total = rows_ref.shape[0], rows_ref.shape[1]
    recordings = pick_ref.shape[0]
    length = total // recordings
    patches = length - 2 * HALO
    reach = left_ref.shape[1]
    live = live_ref[...] > 0

    def put(chunk, offset, row):
        piece = chunk[:, offset : offset + SAMP]
        low_ref[pl.ds(row * lines, lines), :] = piece[:, :128]
        high_ref[pl.ds(row * lines, lines), :] = jnp.concatenate(
            [piece[:, 128:], jnp.zeros((lines, 256 - SAMP), jnp.float32)], axis=1
        )

    def kept(block):
        return jnp.where(live, block.astype(jnp.float32), 0.0)

    blank = jnp.zeros((2 * lines, 128), jnp.float32)
    for part in (low_ref, high_ref):
        part[pl.ds(0, 2 * lines), :] = blank
        part[pl.ds((length - 2) * lines, 2 * lines), :] = blank
    left = kept(left_ref[...])
    right = kept(right_ref[...])
    for q in range(6):
        put(left, reach - (6 - q) * SAMP, 2 + q)
        put(right, q * SAMP, HALO + patches + q)
    period = 16

    def cut(step, carry):
        start = pl.multiple_of(step * (period * SAMP), 128)
        block = kept(signal_ref[:, pl.ds(start, period * SAMP)])
        for q in range(period):
            put(block, q * SAMP, HALO + step * period + q)
        return carry

    lax.fori_loop(0, patches // period, cut, 0)

    def pick(item, carry):
        kind, recording = item // recordings, item % recordings
        line = recording * types + pick_ref[recording, kind]
        place = pl.ds(pl.multiple_of(recording * length, 16), length)
        low = low_ref[pl.ds(line, length, stride=lines), :]
        high = high_ref[pl.ds(line, length, stride=lines), :]
        rows_ref[kind, place, 0:128] = low.astype(jnp.bfloat16)
        rows_ref[kind, place, 128:DEPTH] = high[:, : DEPTH - 128].astype(jnp.bfloat16)
        return carry

    lax.fori_loop(0, types * recordings, pick, 0)


def encode_kernel(
    pick_ref, live_ref, signal_ref, left_ref, right_ref, taps_ref, mix_ref, out_ref,
    rows_ref, low_ref, high_ref, held, wide, encoded, send, recv, second, local,
):
    recordings = pick_ref.shape[0]
    types, total = rows_ref.shape[0], rows_ref.shape[1]
    length = total // recordings
    patches = length - 2 * HALO
    half = types // 2
    me = lax.axis_index("rec")
    pair, parity = me // 2, me % 2
    partner = 2 * pair + (1 - parity)

    square = half == 4
    if square:
        side, over = pair + 1 - 2 * (pair % 2), (pair + 2) % 4
        order, peers = [pair, side, over, 3 - pair], [side, over]
    else:
        order = [(pair + h) % half for h in range(half)]
        peers = [(pair + half - d) % half for d in range(1, half)]
    near = [2 * base + parity for base in order]
    far = [2 * base + (1 - parity) for base in order]
    targets = [partner] + [2 * peer + parity for peer in peers]

    barrier = pltpu.get_barrier_semaphore()
    for target in targets:
        pl.semaphore_signal(barrier, inc=1, device_id={"rec": target}, device_id_type=MESH)
    pl.semaphore_wait(barrier, len(targets))

    sends = []

    def push(source, destination, target, semaphore):
        copy = pltpu.make_async_remote_copy(
            src_ref=source,
            dst_ref=destination,
            send_sem=send.at[len(sends)],
            recv_sem=semaphore,
            device_id={"rec": target},
            device_id_type=MESH,
        )
        copy.start()
        sends.append(copy)

    for target in targets[1:] + targets[:1]:
        push(taps_ref, held.at[me], target, recv.at[me])
    keep = pltpu.make_async_copy(taps_ref, held.at[me], local)
    keep.start()
    edge = jnp.zeros((8, wide.shape[2]), jnp.float32)
    for slot in range(2):
        wide[slot, 0:8, :] = edge
        wide[slot, 8 + length : 16 + length, :] = edge
    position = lax.broadcasted_iota(jnp.int32, (length, EMB), 0) - HALO + me * patches
    inside = jnp.logical_and(position >= 0, position < types * patches)
    cut_rows(
        pick_ref, live_ref, signal_ref, left_ref, right_ref, rows_ref, low_ref, high_ref
    )
    keep.wait()

    def conv(values, weights, slot):
        wide[slot, 8 : 8 + length, :] = jnp.dot(
            values, weights, preferred_element_type=jnp.float32
        )
        taps = weights.shape[1] // EMB
        first = 8 - taps // 2
        result = wide[slot, first : first + length, 0:EMB]
        for k in range(1, taps):
            result = result + wide[slot, first + k : first + k + length, k * EMB : (k + 1) * EMB]
        return jax.nn.gelu(result)

    depth_count = (taps_ref.shape[0] - DEPTH) // EMB

    def encode(source):
        def one(recording, slot):
            start = pl.multiple_of(recording * length, 16)
            patch_rows = rows_ref[source, pl.ds(start, length), :]
            current = conv(patch_rows, held[source, 0:DEPTH, :], slot)
            current = jnp.where(inside, current, 0.0).astype(jnp.bfloat16)
            for layer in range(depth_count):
                base = DEPTH + layer * EMB
                update = conv(current, held[source, base : base + EMB, :], slot)
                current = current.astype(jnp.float32) + update
                current = jnp.where(inside, current, 0.0).astype(jnp.bfloat16)
            encoded[
                pl.ds(pl.multiple_of(recording * patches, 16), patches),
                pl.ds(pl.multiple_of(source * EMB, EMB), EMB),
            ] = current[HALO : HALO + patches]

        def two(step, carry):
            one(2 * step, 0)
            one(2 * step + 1, 1)
            return carry

        lax.fori_loop(0, recordings // 2, two, 0)

    def await_block(block, semaphore):
        pltpu.make_async_remote_copy(
            src_ref=block,
            dst_ref=block,
            send_sem=send.at[0],
            recv_sem=semaphore,
            device_id={"rec": partner},
            device_id_type=MESH,
        ).wait_recv()

    def arrived(slot):
        await_block(held.at[slot], recv.at[slot])

    def forward(slot):
        push(held.at[slot], held.at[slot], partner, recv.at[slot])

    if square:
        split = taps_ref.shape[0] // 32 * 16
        rest = taps_ref.shape[0] - split

        def upper(slot):
            return held.at[slot, pl.ds(0, split)]

        def lower(slot):
            return held.at[slot, pl.ds(split, rest)]

        encode(near[0])
        arrived(near[1])
        push(upper(near[1]), upper(near[1]), targets[2], recv.at[near[1]])
        arrived(near[2])
        push(lower(near[2]), lower(near[2]), targets[1], second)
        forward(near[1])
        forward(near[2])
        arrived(far[0])
        encode(far[0])
        encode(near[1])
        await_block(upper(near[3]), recv.at[near[3]])
        await_block(lower(near[3]), second)
        forward(near[3])
        arrived(far[1])
        encode(far[1])
        encode(near[2])
        arrived(far[2])
        encode(far[2])
        encode(near[3])
        arrived(far[3])
        encode(far[3])
    else:
        for h in range(half):
            if h > 0:
                arrived(near[h])
                forward(near[h])
            encode(near[h])
            arrived(far[h])
            encode(far[h])

    block = 2 * EMB

    def mix(step, carry):
        rows = pl.ds(pl.multiple_of(step * block, block), block)
        out_ref[rows, :] = jnp.dot(
            encoded[rows, :], mix_ref[...], preferred_element_type=jnp.float32
        ).astype(jnp.bfloat16)
        return carry

    lax.fori_loop(0, recordings * patches // block, mix, 0)
    for copy in sends:
        copy.wait_send()


def tail_kernel(
    part_ref, gain_ref, head_ref, extra_ref, out_ref,
    landed, column, spread, send1, recv1, send2, recv2, send3, recv3,
):
    columns, rows = part_ref.shape[0], part_ref.shape[1]
    groups = out_ref.shape[0]
    mine, me = lax.axis_index("chan"), lax.axis_index("rec")
    barrier = pltpu.get_barrier_semaphore()
    for d in range(1, columns):
        pl.semaphore_signal(
            barrier, inc=1, device_id={"chan": (mine + d) % columns}, device_id_type=MESH
        )
    for d in range(1, groups):
        pl.semaphore_signal(
            barrier, inc=1, device_id={"rec": (me + d) % groups}, device_id_type=MESH
        )
    pl.semaphore_wait(barrier, columns + groups - 2)

    def scatter(d):
        peer = (mine + d) % columns
        return pltpu.make_async_remote_copy(
            src_ref=part_ref.at[peer],
            dst_ref=landed.at[d],
            send_sem=send1.at[d],
            recv_sem=recv1.at[d],
            device_id={"chan": peer},
            device_id_type=MESH,
        )

    def along_chan(d):
        return pltpu.make_async_remote_copy(
            src_ref=column.at[mine],
            dst_ref=column.at[mine],
            send_sem=send2.at[d],
            recv_sem=recv2.at[d],
            device_id={"chan": (mine + d) % columns},
            device_id_type=MESH,
        )

    def along_rec(d):
        return pltpu.make_async_remote_copy(
            src_ref=column,
            dst_ref=spread.at[me],
            send_sem=send3.at[d],
            recv_sem=recv3.at[d],
            device_id={"rec": (me + d) % groups},
            device_id_type=MESH,
        )

    for d in range(1, columns):
        scatter(d).start()
    summed = part_ref[mine].astype(jnp.float32)
    for d in range(1, columns):
        scatter(d).wait()
        summed = summed + landed[d].astype(jnp.float32)
    average = jnp.mean(summed, axis=-1, keepdims=True)
    centred = summed - average
    variance = jnp.mean(centred * centred, axis=-1, keepdims=True)
    activated = jax.nn.gelu(centred * lax.rsqrt(variance + EPSILON) * gain_ref[...])
    emission = lax.dot_general(
        head_ref[...],
        activated,
        (((1,), (1,)), ((), ())),
        precision=lax.Precision.HIGHEST,
        preferred_element_type=jnp.float32,
    )
    column[mine] = jnp.zeros(column.shape[1:], jnp.float32)
    column[mine, :, 0:rows] = emission + extra_ref[...]
    for d in range(1, columns):
        along_chan(d).start()
    for d in range(1, columns):
        along_chan(d).wait()
    for d in range(1, groups):
        along_rec(d).start()
    out_ref[me] = column[...]
    for d in range(1, groups):
        along_rec(d).wait()
        source = (me + groups - d) % groups
        out_ref[source] = spread[source]


def local(
    signal,
    montage,
    channels,
    lengths,
    boundary,
    conv_in,
    conv_hid,
    mix_weight,
    norm_gain,
    emit_weight,
    trans_within,
    trans_between,
    initial,
):
    groups = lax.axis_size("rec")
    columns = lax.axis_size("chan")
    chan_index = lax.axis_index("chan")
    rec_index = lax.axis_index("rec")
    recordings, _, samples = signal.shape
    patches = samples // SAMP
    features = mix_weight.shape[-1]
    reach = -(-6 * SAMP // 128) * 128
    lines = recordings * groups
    flat = signal.reshape(lines, samples)
    ahead = [(i, i + 1) for i in range(groups - 1)]
    back = [(i + 1, i) for i in range(groups - 1)]
    left = lax.ppermute(flat[:, samples - reach :], "rec", ahead)
    right = lax.ppermute(flat[:, :reach], "rec", back)
    slot_ids = chan_index * groups + jnp.arange(groups, dtype=jnp.int32)
    live = (slot_ids[None, :] < channels[:, None]).astype(jnp.int32).reshape(lines, 1)
    places = jnp.arange(groups, dtype=jnp.int32)
    matches = montage[:, 0, :, None] == places[None, None, :]
    inverse = jnp.sum(jnp.where(matches, places[None, :, None], 0), axis=1)
    length = patches + 2 * HALO
    first = jnp.transpose(conv_in[0, 0], (1, 0, 2)).reshape(SAMP, -1)
    hidden = jnp.transpose(conv_hid[0, 0], (0, 2, 1, 3)).reshape(-1, first.shape[1])
    blank = jnp.zeros((DEPTH - SAMP, first.shape[1]), jnp.bfloat16)
    taps = jnp.concatenate([first, blank, hidden], axis=0)
    partial = pl.pallas_call(
        encode_kernel,
        out_shape=jax.ShapeDtypeStruct((recordings * patches, features), jnp.bfloat16),
        in_specs=[pl.BlockSpec(memory_space=pltpu.SMEM)] + [vmem_spec()] * 6,
        out_specs=vmem_spec(),
        scratch_shapes=[
            pltpu.VMEM((groups, recordings * length, DEPTH), jnp.bfloat16),
            pltpu.VMEM((length * lines, 128), jnp.float32),
            pltpu.VMEM((length * lines, 128), jnp.float32),
            pltpu.VMEM((groups,) + taps.shape, jnp.bfloat16),
            pltpu.VMEM((2, length + 16, taps.shape[1]), jnp.float32),
            pltpu.VMEM((recordings * patches, groups * EMB), jnp.bfloat16),
            pltpu.SemaphoreType.DMA((groups + 2,)),
            pltpu.SemaphoreType.DMA((groups,)),
            pltpu.SemaphoreType.DMA,
            pltpu.SemaphoreType.DMA,
        ],
        compiler_params=pltpu.CompilerParams(
            collective_id=0, has_side_effects=True, vmem_limit_bytes=VMEM_LIMIT
        ),
    )(inverse, live, flat, left, right, taps, mix_weight[:, 0].reshape(groups * EMB, features))

    rows = recordings * patches // columns
    padded = -(-rows // 128) * 128
    cross = lax.dynamic_slice_in_dim(boundary.reshape(-1), chan_index * rows, rows)
    cross = (cross == 1).astype(jnp.float32)
    extra = jnp.pad(cross[None], ((STATES, 2), (0, 0)))
    head = jnp.pad(emit_weight.T, ((0, 8 - STATES), (0, 0)))
    field = pl.pallas_call(
        tail_kernel,
        out_shape=jax.ShapeDtypeStruct((groups, columns, 8, padded), jnp.float32),
        in_specs=[vmem_spec()] * 4,
        out_specs=vmem_spec(),
        scratch_shapes=[
            pltpu.VMEM((columns, rows, features), jnp.bfloat16),
            pltpu.VMEM((columns, 8, padded), jnp.float32),
            pltpu.VMEM((groups, columns, 8, padded), jnp.float32),
        ]
        + [pltpu.SemaphoreType.DMA((count,)) for count in (columns, columns) * 2 + (groups, groups)],
        compiler_params=pltpu.CompilerParams(
            collective_id=1, has_side_effects=True, vmem_limit_bytes=VMEM_LIMIT
        ),
    )(partial.reshape(columns, rows, features), norm_gain[None], head, extra)

    wide = LANES // groups
    steps = patches // wide
    field = field[:, :, : STATES + 1, :rows]
    field = jnp.transpose(field, (0, 2, 1, 3)).reshape(
        groups, STATES + 1, recordings, wide, steps
    )
    field = jnp.transpose(field, (1, 4, 2, 0, 3)).reshape(STATES + 1, steps, recordings, LANES)
    history, total = crf(field, lengths, trans_within, trans_between, initial)
    own = lax.dynamic_slice_in_dim(history, rec_index * wide, wide, axis=3)
    filtered = jnp.transpose(own, (2, 1, 3, 0)).reshape(recordings, STATES, patches)
    return filtered, total[:, LANES - 1] / lengths.astype(jnp.float32)


def solution(mesh):
    placed = (
        P(None, "chan", "rec"),
        P(None, "chan", None),
        P(),
        P(),
        P(None, "rec"),
        P("rec", "chan", None, None, None),
        P("rec", "chan", None, None, None, None),
        P(None, "chan", None, None),
        P(),
        P(),
        P(),
        P(),
        P(),
    )
    return jax.shard_map(
        local, mesh=mesh, in_specs=placed, out_specs=(P(None, None, "rec"), P()), check_vma=False
    )
```
